256 devices in a mesh: pair: 32 (over z, y_hi, core), band: 8 (over y_lo, x).
Axes of the slice: x: 4, y: 4 (y_hi: 2, y_lo: 2; y = y_hi * 2 + y_lo), z: 8, core: 2. Of those that a mesh axis runs over, the one named last changes fastest.
Arguments:
- spectra: bfloat16 [2, 512, 4096, 256], P(None, 'band', 'pair'), may hold values from -600 to 600, as said below
- live: int32 [4096], P('pair'), may hold values 0 or 1
Outputs:
- correlations: float32 [524288, 256], P(('pair', 'band'))
The draws below stay inside these ranges and needn't reach their ends.
Inputs may be any that keep to these rules, and one draw needn't show every extreme that they name: `spectra`: finite values.
All inputs are finite; a program needn't handle non-finite values. No bound on the sum of `live` on one device may be relied on, other than what follows from the above.
Results may differ from the reference program's by a relative error of at most 0.017.
Values may be sent and summed in bfloat16 or wider, within the bound.
No kernel may reach another device: no remote copies, remote signals or barrier semaphores. Data moves between devices by JAX's collectives and lax.ppermute only.
A program may use at most 128 MiB of HBM per device.

```python
import jax
import jax.numpy as jnp
from jax import lax

CH = 128
W = 256
NF = 512
LAGS = 256
NFFT = 2048
K0 = 64
OFFSET = 5
NCH = 4096
NPAIRS = 524288
N_PAIR = 32


def draw_spectra(key, part):
    key = jax.random.fold_in(key, 11)
    base_key, window_key, freq_key = jax.random.split(key, 3)
    shape = (2, NF, NCH, W)
    base = jnp.clip(jax.random.normal(base_key, shape, jnp.float32), -6.0, 6.0)
    window_scale = jnp.exp(jax.random.uniform(window_key, (1, 1, NCH, W), jnp.float32) * jnp.log(10.0))
    freq_scale = jnp.exp(jax.random.uniform(freq_key, (1, NF, NCH, 1), jnp.float32) * jnp.log(10.0))
    return (base * window_scale * freq_scale).astype(jnp.bfloat16)


def plant(array, stream_key, low, high):
    place = [jax.random.randint(jax.random.fold_in(stream_key, axis), (), 0, length) for axis, length in enumerate(array.shape)]
    widest = array.shape.index(max(array.shape))
    next_to = place[:widest] + [(place[widest] + 1) % array.shape[widest]] + place[widest + 1:]
    return array.at[tuple(place)].set(low).at[tuple(next_to)].set(high)


def setup_inputs(seed: int = 0) -> dict:
    arg_keys = jax.random.split(jax.random.key(seed), 3)
    return {
        "spectra": draw_spectra(jax.random.fold_in(arg_keys[2], 71), 0),
        "live": plant((jax.random.randint(arg_keys[1], (NCH,), 0, 8) < 7).astype(jnp.int32), jax.random.fold_in(arg_keys[1], 1), 0, 1),
    }


def lag_tables(first, count, lags):
    freq = first + jnp.arange(count, dtype=jnp.int32)
    lag_index = jnp.arange(lags, dtype=jnp.int32) - lags // 2
    phase = freq[:, None] * lag_index[None, :] % NFFT
    angle = phase.astype(jnp.float32) * (2.0 * jnp.pi / NFFT)
    return jnp.stack([jnp.cos(angle), -jnp.sin(angle)]).astype(jnp.bfloat16)

def reference(spectra, live):
    masked = spectra.astype(jnp.float32) * live.astype(jnp.float32)[None, None, :, None]
    amplitude = jnp.sqrt(lax.optimization_barrier(jnp.mean(masked[0] * masked[0] + masked[1] * masked[1], axis=2)) + 1e-06)
    white = (masked / amplitude[None, :, :, None]).astype(jnp.bfloat16)
    rolled = jnp.roll(white, -OFFSET * CH, axis=2)
    table = lag_tables(K0, NF, LAGS).astype(jnp.float32)

    def one_block(block):
        start = (block * CH).astype(jnp.int32)
        own = lax.dynamic_slice_in_dim(white, start, CH, 2).astype(jnp.float32)
        other = lax.dynamic_slice_in_dim(rolled, start, CH, 2).astype(jnp.float32)
        product = jnp.einsum('sfaw,tfbw->stfab', own, other)
        real_part = (product[0, 0] + product[1, 1]) / jnp.sqrt(jnp.float32(W))
        imag_part = (product[1, 0] - product[0, 1]) / jnp.sqrt(jnp.float32(W))
        cross = jnp.stack([real_part, imag_part]).reshape(2, NF, CH * CH).astype(jnp.bfloat16)
        summed = jnp.einsum('sfp,sfl->pl', cross.astype(jnp.float32), table)
        return summed / jnp.sqrt(jnp.float32(NF))
    blocks = lax.map(one_block, jnp.arange(N_PAIR, dtype=jnp.int32))
    return blocks.reshape(NPAIRS, LAGS)
```

```python
import functools

import jax
import jax.numpy as jnp
from jax import lax
from jax.experimental import pallas as pl
from jax.experimental.pallas import tpu as pltpu
from jax.sharding import PartitionSpec as P

LAGS = 256
NFFT = 2048
K0 = 64
OFFSET = 5
CHUNK = 8
STEP = 2


def shift(value, axis, steps):
    count = lax.axis_size(axis)
    pairs = [(source, (source + steps) % count) for source in range(count)]
    return lax.ppermute(value, axis, pairs)


def whiten_kernel(x_ref, live_ref, o_ref):
    live = live_ref[...]
    windows = x_ref.shape[3]
    for f in range(x_ref.shape[1]):
        real = x_ref[0, f].astype(jnp.float32)
        imag = x_ref[1, f].astype(jnp.float32)
        power = jnp.sum(real * real + imag * imag, axis=1, keepdims=True) * (1.0 / windows)
        scale = live * lax.rsqrt(live * live * power + 1e-06)
        o_ref[f, 0] = (real * scale).astype(jnp.bfloat16)
        o_ref[f, 1] = (imag * scale).astype(jnp.bfloat16)


def whiten(spectra, live, chunk):
    _, _, channels, windows = spectra.shape
    steps = CHUNK // STEP
    return pl.pallas_call(
        whiten_kernel,
        grid=(steps,),
        in_specs=[
            pl.BlockSpec((2, STEP, channels, windows), lambda i: (0, chunk * steps + i, 0, 0)),
            pl.BlockSpec((channels, 1), lambda i: (0, 0)),
        ],
        out_specs=pl.BlockSpec((STEP, 2, channels, windows), lambda i: (i, 0, 0, 0)),
        out_shape=jax.ShapeDtypeStruct((CHUNK, 2, channels, windows), jnp.bfloat16),
        cost_estimate=pl.CostEstimate(
            flops=8 * 2 * CHUNK * channels * windows,
            bytes_accessed=8 * CHUNK * channels * windows,
            transcendentals=0,
        ),
        name="whiten",
    )(spectra, live)


def cross_kernel(x_ref, y_ref, o_ref, acc):
    count, _, channels, windows = x_ref.shape
    depth = 2 * count
    norm = 1.0 / windows**0.5
    for f in range(count):
        x = x_ref[f].reshape(2 * channels, windows)
        y = y_ref[f].reshape(2 * channels, windows)
        product = lax.dot_general(
            x, y, (((1,), (1,)), ((), ())), preferred_element_type=jnp.float32
        )
        low, high = product[:channels], product[channels:]
        real = low[:, :channels] + high[:, channels:]
        imag = high[:, :channels] - low[:, channels:]
        acc[pl.ds(f, channels, stride=depth), :] = real * norm
        acc[pl.ds(count + f, channels, stride=depth), :] = imag * norm
    o_ref[...] = acc[...].astype(jnp.bfloat16)


def cross(x, y):
    count, _, channels, windows = x.shape
    rows = channels * 2 * count
    return pl.pallas_call(
        cross_kernel,
        out_shape=jax.ShapeDtypeStruct((rows, channels), jnp.bfloat16),
        scratch_shapes=[pltpu.VMEM((rows, channels), jnp.float32)],
        cost_estimate=pl.CostEstimate(
            flops=8 * count * channels * channels * windows,
            bytes_accessed=8 * count * channels * windows + 2 * rows * channels,
            transcendentals=0,
        ),
        compiler_params=pltpu.CompilerParams(vmem_limit_bytes=32 * 1024 * 1024),
        name="cross",
    )(x, y)


def lags_kernel(parts, norm, *refs):
    piece_refs, table_ref, o_ref = refs[:parts], refs[parts], refs[parts + 1]
    bands, rows, channels = piece_refs[0].shape
    depth = 2 * CHUNK
    for a in range(rows // depth):
        columns = jnp.concatenate(
            [ref[band, a * depth : (a + 1) * depth, :] for ref in piece_refs for band in range(bands)],
            axis=0,
        )
        total = lax.dot_general(
            columns, table_ref[...], (((0,), (0,)), ((), ())), preferred_element_type=jnp.float32
        )
        o_ref[a * channels : (a + 1) * channels, :] = (total * norm).astype(o_ref.dtype)


def to_lags(pieces, table, norm, dtype):
    bands, rows, channels = pieces[0].shape
    pairs = rows // (2 * CHUNK) * channels
    lags = table.shape[1]
    return pl.pallas_call(
        functools.partial(lags_kernel, len(pieces), norm),
        out_shape=jax.ShapeDtypeStruct((pairs, lags), dtype),
        cost_estimate=pl.CostEstimate(
            flops=2 * pairs * lags * table.shape[0],
            bytes_accessed=2 * pairs * table.shape[0] + 4 * pairs * lags,
            transcendentals=0,
        ),
        compiler_params=pltpu.CompilerParams(vmem_limit_bytes=32 * 1024 * 1024),
        name="to_lags",
    )(*pieces, table)


def lag_table(chunks, bands, freq_local):
    chunk = jnp.asarray(chunks, jnp.int32)[:, None, None]
    band = jnp.arange(bands, dtype=jnp.int32)[None, :, None]
    inner = jnp.arange(CHUNK, dtype=jnp.int32)[None, None, :]
    freq = K0 + band * freq_local + chunk * CHUNK + inner
    lag_index = jnp.arange(LAGS, dtype=jnp.int32) - LAGS // 2
    phase = freq[..., None] * lag_index % NFFT
    angle = phase.astype(jnp.float32) * (2.0 * jnp.pi / NFFT)
    table = jnp.stack([jnp.cos(angle), -jnp.sin(angle)], axis=2)
    return table.reshape(-1, LAGS).astype(jnp.bfloat16)


def local(spectra, live):
    _, freq_local, channels, windows = spectra.shape
    bands = lax.axis_size("band")
    chunks = freq_local // CHUNK
    up = list(range(chunks // 2))
    down = list(range(chunks // 2, chunks))
    norm = 1.0 / float(freq_local * bands) ** 0.5
    mask = live.astype(jnp.float32)[:, None]
    white = [whiten(spectra, mask, chunk) for chunk in range(chunks)]

    def exchange(own, other):
        value = cross(own, other).reshape(bands, -1, channels)
        return lax.all_to_all(value, "band", 0, 0)

    up_pieces, down_pieces = [], []
    up_got, down_got = [], []
    for u, d in zip(up, down):
        send_up, send_down = white[u], white[d]
        if len(up_got) >= 2:
            send_up, _ = lax.optimization_barrier((send_up, up_got[-2]))
            send_down, _ = lax.optimization_barrier((send_down, down_got[-2]))
        up_got.append(shift(send_up, "pair", OFFSET))
        down_got.append(shift(send_down, "pair", -OFFSET))
    for step, (u, d) in enumerate(zip(up, down)):
        up_pieces.append(exchange(up_got[step], white[u]))
        down_pieces.append(exchange(white[d], down_got[step]))
    back = to_lags(up_pieces, lag_table(up, bands, freq_local), norm, jnp.bfloat16)
    back = shift(back, "pair", -OFFSET)
    here = to_lags(down_pieces, lag_table(down, bands, freq_local), norm, jnp.float32)
    return here + back.astype(jnp.float32)


def solution(mesh):
    in_specs = (P(None, "band", "pair", None), P("pair"))
    out_specs = P(("pair", "band"), None)
    return jax.shard_map(local, mesh=mesh, in_specs=in_specs, out_specs=out_specs, check_vma=False)
```

```python
import functools

import jax
import jax.numpy as jnp
from jax import lax
from jax.experimental import pallas as pl
from jax.experimental.pallas import tpu as pltpu
from jax.sharding import PartitionSpec as P

LAGS = 256
NFFT = 2048
K0 = 64
OFFSET = 5
STEP = 4
GROUPS = (("down", 1), ("up", 1), ("up", 1), ("down", 1), ("up", 1), ("up", 1), ("down", 1), ("up", 1))
WHITEN = (2, 6)
PLAN = (
    ("send", 0),
    ("send", 1),
    ("send", 2),
    ("send", 3),
    ("send", 4),
    ("join", (0, 1), "t", "s"),
    ("send", 5, "v0"),
    ("join", (2, 4), "v0", "g3"),
    ("send", 7, "p0"),
    ("send", 6, "g5"),
    ("join", (5,), "v1", "p0"),
    ("join", (7,), "v2", "p1"),
    ("join", (3, 6), "v3", "p2"),
)


def whiten_kernel(starts, x_ref, live_ref, *o_refs):
    live = live_ref[...]
    windows = x_ref.shape[3]
    step = pl.program_id(0)

    def write(o_ref):
        for f in range(STEP):
            real = x_ref[0, f].astype(jnp.float32)
            imag = x_ref[1, f].astype(jnp.float32)
            power = jnp.sum(real * real + imag * imag, axis=1, keepdims=True) * (1.0 / windows)
            scale = live * lax.rsqrt(live * live * power + 1e-06)
            o_ref[f, 0] = (real * scale).astype(jnp.bfloat16)
            o_ref[f, 1] = (imag * scale).astype(jnp.bfloat16)

    for k, o_ref in enumerate(o_refs):
        pl.when((step >= starts[k]) & (step < starts[k + 1]))(functools.partial(write, o_ref))


def whiten(spectra, live, first, counts):
    _, _, channels, windows = spectra.shape
    steps = [count // STEP for count in counts]
    starts = [sum(steps[:k]) for k in range(len(steps) + 1)]

    def out_block(k):
        return lambda i: (jnp.clip(i - starts[k], 0, steps[k] - 1), 0, 0, 0)

    return pl.pallas_call(
        functools.partial(whiten_kernel, starts),
        grid=(starts[-1],),
        in_specs=[
            pl.BlockSpec((2, STEP, channels, windows), lambda i: (0, first // STEP + i, 0, 0)),
            pl.BlockSpec((channels, 1), lambda i: (0, 0)),
        ],
        out_specs=[
            pl.BlockSpec((STEP, 2, channels, windows), out_block(k)) for k in range(len(counts))
        ],
        out_shape=[
            jax.ShapeDtypeStruct((count, 2, channels, windows), jnp.bfloat16) for count in counts
        ],
        cost_estimate=pl.CostEstimate(
            flops=16 * sum(counts) * channels * windows,
            bytes_accessed=8 * sum(counts) * channels * windows,
            transcendentals=0,
        ),
        name="whiten",
    )(spectra, live)


def cross_kernel(shapes, pick_ref, *refs):
    *refs, o_ref, acc = refs
    bands = o_ref.shape[0]
    place = 0
    for sources in shapes:
        x_ref, y_refs, refs = refs[0], refs[1 : 1 + sources], refs[1 + sources :]
        count, _, channels, windows = x_ref.shape
        depth = 2 * count
        norm = 1.0 / windows**0.5
        for f in range(count):
            x = x_ref[f].reshape(2 * channels, windows)
            y = y_refs[0][f]
            if sources > 1:
                y = jnp.where(pick_ref[0] > 0, y_refs[1][f], y)
            y = y.reshape(2 * channels, windows)
            product = lax.dot_general(
                x, y, (((1,), (1,)), ((), ())), preferred_element_type=jnp.float32
            )
            low, high = product[:channels], product[channels:]
            real = low[:, :channels] + high[:, channels:]
            imag = high[:, :channels] - low[:, channels:]
            acc[pl.ds(f, channels, stride=depth), :] = real * norm
            acc[pl.ds(count + f, channels, stride=depth), :] = imag * norm
        rows = channels * depth // bands
        for band in range(bands):
            part = acc[band * rows : (band + 1) * rows, :]
            o_ref[band, place : place + rows, :] = part.astype(jnp.bfloat16)
        place += rows


def cross(groups, pick, bands):
    channels = groups[0][0].shape[2]
    rows = [channels * 2 * x.shape[0] for x, _ in groups]
    work = sum(x.size for x, _ in groups)
    return pl.pallas_call(
        functools.partial(cross_kernel, [len(ys) for _, ys in groups]),
        in_specs=[pl.BlockSpec(memory_space=pltpu.SMEM)]
        + [pl.BlockSpec(memory_space=pltpu.VMEM)] * sum(1 + len(ys) for _, ys in groups),
        out_shape=jax.ShapeDtypeStruct((bands, sum(rows) // bands, channels), jnp.bfloat16),
        scratch_shapes=[pltpu.VMEM((max(rows), channels), jnp.float32)],
        compiler_params=pltpu.CompilerParams(vmem_limit_bytes=40 * 1024 * 1024),
        cost_estimate=pl.CostEstimate(
            flops=4 * work * channels, bytes_accessed=5 * work, transcendentals=0
        ),
        name="cross",
    )(pick, *[ref for x, ys in groups for ref in (x, *ys)])


def lags_kernel(norm, places, *refs):
    *piece_refs, table_ref, o_ref = refs
    rows, channels = o_ref.shape[0], piece_refs[0].shape[2]
    for a in range(rows // channels):
        columns = []
        for ref, (place, depth) in zip(piece_refs, places):
            start = place + a * depth
            columns += [ref[band, start : start + depth, :] for band in range(ref.shape[0])]
        total = lax.dot_general(
            jnp.concatenate(columns, axis=0),
            table_ref[...],
            (((0,), (0,)), ((), ())),
            preferred_element_type=jnp.float32,
        )
        o_ref[a * channels : (a + 1) * channels, :] = (total * norm).astype(o_ref.dtype)


def to_lags(pieces, table, norm, dtype):
    bands, _, channels = pieces[0][0].shape
    pairs = channels * channels // bands
    lags = table.shape[1]
    return pl.pallas_call(
        functools.partial(lags_kernel, norm, [(place, depth) for _, place, depth in pieces]),
        out_shape=jax.ShapeDtypeStruct((pairs, lags), dtype),
        compiler_params=pltpu.CompilerParams(vmem_limit_bytes=32 * 1024 * 1024),
        cost_estimate=pl.CostEstimate(
            flops=2 * pairs * table.size,
            bytes_accessed=2 * pairs * table.shape[0] + 4 * pairs * lags,
            transcendentals=0,
        ),
        name="to_lags",
    )(*[piece for piece, _, _ in pieces], table)


def lag_table(first, count, bands, freq_local):
    band = jnp.arange(bands, dtype=jnp.int32)[:, None]
    freq = K0 + band * freq_local + first + jnp.arange(count, dtype=jnp.int32)
    lag_index = jnp.arange(LAGS, dtype=jnp.int32) - LAGS // 2
    phase = freq[..., None] * lag_index % NFFT
    angle = phase.astype(jnp.float32) * (2.0 * jnp.pi / NFFT)
    table = jnp.stack([jnp.cos(angle), -jnp.sin(angle)], axis=1)
    return table.reshape(-1, LAGS).astype(jnp.bfloat16)


def routes(blocks):
    behind, ahead, third, back = [], [], [], []
    for i in range(blocks):
        partner = (i + OFFSET) % blocks
        place = (partner, partner - 2, i + 1, partner + 2)[i % 4] % blocks
        behind.append((partner, i))
        ahead.append((i, place))
        back.append((place, i))
        if place != partner:
            third.append((partner, place))
    return behind, ahead, third, back


def local(spectra, live):
    _, freq_local, channels, windows = spectra.shape
    bands = lax.axis_size("band")
    behind, ahead, third, back = routes(lax.axis_size("pair"))
    norm = 1.0 / float(freq_local * bands) ** 0.5
    mask = live.astype(jnp.float32)[:, None]
    pick = (lax.axis_index("pair") % 4 != 1).astype(jnp.int32)[None]
    counts = [eighths * freq_local // 8 for _, eighths in GROUPS]
    firsts = [sum(counts[:k]) for k in range(len(counts))]

    def after(own, earlier):
        return lax.optimization_barrier((own, earlier))[0]

    white = []
    for members in WHITEN:
        source = after(spectra, white[-1]) if white else spectra
        white += whiten(source, mask, firsts[len(white)], counts[len(white) : len(white) + members])

    table = {
        way: jnp.concatenate(
            [
                lag_table(firsts[k], counts[k], bands, freq_local)
                for kind, what, *_ in PLAN
                if kind == "join"
                for k in what
                if GROUPS[k][0] == way
            ]
        )
        for way in ("up", "down")
    }
    there = {"t": table["up"], "s": table["down"]}
    arrived = {}
    pieces = {"up": [], "down": []}
    for kind, what, *needs in PLAN:
        if kind == "send":
            way, own = GROUPS[what][0], white[what]
            sent = own
            for need in needs:
                sent = after(sent, there[need])
            moved = lax.ppermute(sent, "pair", ahead if way == "up" else behind)
            there[f"g{what}"] = moved
            if way == "up":
                arrived[what] = (moved, [own, lax.ppermute(sent, "pair", third)])
            else:
                arrived[what] = (own, [moved])
            continue
        factors = [arrived[k] for k in what]
        for need in needs:
            factors[0] = (after(factors[0][0], there[need]), factors[0][1])
        value = cross(factors, pick, bands)
        piece = lax.all_to_all(value, "band", 0, 0)
        number = sum(name[0] == "v" for name in there)
        there[f"v{number}"], there[f"p{number}"] = value, piece
        place = 0
        for k in what:
            way = GROUPS[k][0]
            pieces[way].append((piece, place, 2 * counts[k]))
            place += channels // bands * 2 * counts[k]
    far = to_lags(pieces["up"], table["up"], norm, jnp.bfloat16)
    far = lax.ppermute(far, "pair", back)
    near = to_lags(pieces["down"], table["down"], norm, jnp.float32)
    return near + far.astype(jnp.float32)


def solution(mesh):
    in_specs = (P(None, "band", "pair", None), P("pair"))
    out_specs = P(("pair", "band"), None)
    return jax.shard_map(local, mesh=mesh, in_specs=in_specs, out_specs=out_specs, check_vma=False)
```

```python
import functools

import jax
import jax.numpy as jnp
from jax import lax
from jax.experimental import pallas as pl
from jax.experimental.pallas import tpu as pltpu
from jax.sharding import PartitionSpec as P

LAGS = 256
NFFT = 2048
K0 = 64
OFFSET = 5
STEP = 8
GROUPS = (("down", 1), ("up", 1), ("up", 1), ("down", 1), ("up", 1), ("up", 1), ("down", 1), ("up", 1))
WHITEN = (2, 3, 3)
PLAN = (
    ("send", 0),
    ("send", 1),
    ("third", 1),
    ("send", 2),
    ("third", 2),
    ("send", 3),
    ("send", 4),
    ("third", 4),
    ("join", (0, 1), "t", "s"),
    ("send", 5, "v0"),
    ("third", 5, "v0"),
    ("join", (2, 4), "v0", "g3"),
    ("send", 7, "p0"),
    ("third", 7, "p0"),
    ("send", 6, "g5"),
    ("join", (5,), "v1", "p0"),
    ("join", (7,), "v2", "p1"),
    ("join", (3, 6), "v3", "p2"),
)


def row_sums(x):
    ones = jnp.ones((x.shape[1], 128), jnp.bfloat16)
    high = x.astype(jnp.bfloat16)
    low = (x - high.astype(jnp.float32)).astype(jnp.bfloat16)
    return jnp.dot(high, ones, preferred_element_type=jnp.float32) + jnp.dot(
        low, ones, preferred_element_type=jnp.float32
    )


def whiten_kernel(starts, x_ref, live_ref, *o_refs):
    channels, windows = x_ref.shape[2:]
    step = pl.program_id(0)
    rows = lax.broadcasted_iota(jnp.int32, (channels, channels), 0)
    columns = lax.broadcasted_iota(jnp.int32, (channels, channels), 1)
    live = row_sums(jnp.where(rows == columns, live_ref[...].astype(jnp.float32), 0.0))

    def write(o_ref):
        for f in range(STEP):
            real = x_ref[0, f].astype(jnp.float32)
            imag = x_ref[1, f].astype(jnp.float32)
            power = row_sums(real * real + imag * imag) * (1.0 / windows)
            scale = live * lax.rsqrt(live * live * power + 1e-06)
            for lane in range(0, windows, 128):
                part = slice(lane, lane + 128)
                o_ref[f, 0, :, part] = (real[:, part] * scale).astype(jnp.bfloat16)
                o_ref[f, 1, :, part] = (imag[:, part] * scale).astype(jnp.bfloat16)

    for k, o_ref in enumerate(o_refs):
        pl.when((step >= starts[k]) & (step < starts[k + 1]))(functools.partial(write, o_ref))


def whiten(spectra, live, first, counts):
    _, _, channels, windows = spectra.shape
    steps = [count // STEP for count in counts]
    starts = [sum(steps[:k]) for k in range(len(steps) + 1)]

    def out_block(k):
        return lambda i: (jnp.clip(i - starts[k], 0, steps[k] - 1), 0, 0, 0)

    return pl.pallas_call(
        functools.partial(whiten_kernel, starts),
        grid=(starts[-1],),
        in_specs=[
            pl.BlockSpec((2, STEP, channels, windows), lambda i: (0, first // STEP + i, 0, 0)),
            pl.BlockSpec((1, channels), lambda i: (0, 0)),
        ],
        out_specs=[
            pl.BlockSpec((STEP, 2, channels, windows), out_block(k)) for k in range(len(counts))
        ],
        out_shape=[
            jax.ShapeDtypeStruct((count, 2, channels, windows), jnp.bfloat16) for count in counts
        ],
        cost_estimate=pl.CostEstimate(
            flops=16 * sum(counts) * channels * windows,
            bytes_accessed=8 * sum(counts) * channels * windows,
            transcendentals=0,
        ),
        name="whiten",
    )(spectra, live)


def cross_kernel(shapes, pick_ref, *refs):
    *refs, o_ref, acc = refs
    bands = o_ref.shape[0]
    place = 0
    for sources in shapes:
        x_ref, y_refs, refs = refs[0], refs[1 : 1 + sources], refs[1 + sources :]
        count, _, channels, windows = x_ref.shape
        depth = 2 * count
        norm = 1.0 / windows**0.5
        for f in range(count):
            x = x_ref[f].reshape(2 * channels, windows)
            y = y_refs[0][f]
            if sources > 1:
                y = jnp.where(pick_ref[0] > 0, y_refs[1][f], y)
            y = y.reshape(2 * channels, windows)
            product = lax.dot_general(
                x, y, (((1,), (1,)), ((), ())), preferred_element_type=jnp.float32
            )
            low, high = product[:channels], product[channels:]
            real = low[:, :channels] + high[:, channels:]
            imag = high[:, :channels] - low[:, channels:]
            acc[pl.ds(f, channels, stride=depth), :] = real * norm
            acc[pl.ds(count + f, channels, stride=depth), :] = imag * norm
        rows = channels * depth // bands
        for band in range(bands):
            part = acc[band * rows : (band + 1) * rows, :]
            o_ref[band, place : place + rows, :] = part.astype(jnp.bfloat16)
        place += rows


def cross(groups, pick, bands):
    channels = groups[0][0].shape[2]
    rows = [channels * 2 * x.shape[0] for x, _ in groups]
    work = sum(x.size for x, _ in groups)
    return pl.pallas_call(
        functools.partial(cross_kernel, [len(ys) for _, ys in groups]),
        in_specs=[pl.BlockSpec(memory_space=pltpu.SMEM)]
        + [pl.BlockSpec(memory_space=pltpu.VMEM)] * sum(1 + len(ys) for _, ys in groups),
        out_shape=jax.ShapeDtypeStruct((bands, sum(rows) // bands, channels), jnp.bfloat16),
        scratch_shapes=[pltpu.VMEM((max(rows) + max(rows) // channels, channels), jnp.float32)],
        compiler_params=pltpu.CompilerParams(vmem_limit_bytes=40 * 1024 * 1024),
        cost_estimate=pl.CostEstimate(
            flops=4 * work * channels, bytes_accessed=5 * work, transcendentals=0
        ),
        name="cross",
    )(pick, *[ref for x, ys in groups for ref in (x, *ys)])


def lags_kernel(norm, places, *refs):
    *piece_refs, table_ref, o_ref = refs
    rows, channels = o_ref.shape[0], piece_refs[0].shape[2]
    for a in range(rows // channels):
        columns = []
        for ref, (place, depth) in zip(piece_refs, places):
            start = place + a * depth
            columns += [ref[band, start : start + depth, :] for band in range(ref.shape[0])]
        total = lax.dot_general(
            jnp.concatenate(columns, axis=0),
            table_ref[...],
            (((0,), (0,)), ((), ())),
            preferred_element_type=jnp.float32,
        )
        o_ref[a * channels : (a + 1) * channels, :] = (total * norm).astype(o_ref.dtype)


def to_lags(pieces, table, norm, dtype):
    bands, _, channels = pieces[0][0].shape
    pairs = channels * channels // bands
    lags = table.shape[1]
    return pl.pallas_call(
        functools.partial(lags_kernel, norm, [(place, depth) for _, place, depth in pieces]),
        out_shape=jax.ShapeDtypeStruct((pairs, lags), dtype),
        compiler_params=pltpu.CompilerParams(vmem_limit_bytes=32 * 1024 * 1024),
        cost_estimate=pl.CostEstimate(
            flops=2 * pairs * table.size,
            bytes_accessed=2 * pairs * table.shape[0] + 4 * pairs * lags,
            transcendentals=0,
        ),
        name="to_lags",
    )(*[piece for piece, _, _ in pieces], table)


def lag_table(first, count, bands, freq_local):
    band = jnp.arange(bands, dtype=jnp.int32)[:, None]
    freq = K0 + band * freq_local + first + jnp.arange(count, dtype=jnp.int32)
    lag_index = jnp.arange(LAGS, dtype=jnp.int32) - LAGS // 2
    phase = freq[..., None] * lag_index % NFFT
    angle = phase.astype(jnp.float32) * (2.0 * jnp.pi / NFFT)
    table = jnp.stack([jnp.cos(angle), -jnp.sin(angle)], axis=1)
    return table.reshape(-1, LAGS).astype(jnp.bfloat16)


def routes(blocks):
    behind, ahead, third, back = [], [], [], []
    for i in range(blocks):
        partner = (i + OFFSET) % blocks
        place = (partner, partner - 2, i + 1, partner + 2)[i % 4] % blocks
        behind.append((partner, i))
        ahead.append((i, place))
        back.append((place, i))
        if place != partner:
            third.append((partner, place))
    return behind, ahead, third, back


def local(spectra, live):
    _, freq_local, channels, windows = spectra.shape
    bands = lax.axis_size("band")
    behind, ahead, third, back = routes(lax.axis_size("pair"))
    norm = 1.0 / float(freq_local * bands) ** 0.5
    mask = live[None, :]
    pick = (lax.axis_index("pair") % 4 != 1).astype(jnp.int32)[None]
    counts = [eighths * freq_local // 8 for _, eighths in GROUPS]
    firsts = [sum(counts[:k]) for k in range(len(counts))]

    def after(own, earlier):
        return lax.optimization_barrier((own, earlier))[0]

    white = []
    for members in WHITEN:
        source = after(spectra, white[-1]) if white else spectra
        white += whiten(source, mask, firsts[len(white)], counts[len(white) : len(white) + members])

    table = {
        way: jnp.concatenate(
            [
                lag_table(firsts[k], counts[k], bands, freq_local)
                for kind, what, *_ in PLAN
                if kind == "join"
                for k in what
                if GROUPS[k][0] == way
            ]
        )
        for way in ("up", "down")
    }
    there = {"t": table["up"], "s": table["down"]}
    arrived = {}
    pieces = {"up": [], "down": []}
    for kind, what, *needs in PLAN:
        if kind != "join":
            way, own = GROUPS[what][0], white[what]
            sent = own
            for need in needs:
                sent = after(sent, there[need])
            if kind == "third":
                moved = there[f"y{what}"] = lax.ppermute(sent, "pair", third)
                arrived.setdefault(what, [own, [own]])[1].append(moved)
            elif way == "up":
                moved = there[f"g{what}"] = lax.ppermute(sent, "pair", ahead)
                arrived.setdefault(what, [own, [own]])[0] = moved
            else:
                moved = there[f"g{what}"] = lax.ppermute(sent, "pair", behind)
                arrived[what] = [own, [moved]]
            continue
        factors = [arrived[k] for k in what]
        for need in needs:
            factors[0] = [after(factors[0][0], there[need]), factors[0][1]]
        value = cross(factors, pick, bands)
        piece = lax.all_to_all(value, "band", 0, 0)
        number = sum(name[0] == "v" for name in there)
        there[f"v{number}"], there[f"p{number}"] = value, piece
        place = 0
        for k in what:
            way = GROUPS[k][0]
            pieces[way].append((piece, place, 2 * counts[k]))
            place += channels // bands * 2 * counts[k]
    far = to_lags(pieces["up"], table["up"], norm, jnp.bfloat16)
    far = lax.ppermute(far, "pair", back)
    near = to_lags(pieces["down"], table["down"], norm, jnp.float32)
    return near + far.astype(jnp.float32)


def solution(mesh):
    in_specs = (P(None, "band", "pair", None), P("pair"))
    out_specs = P(("pair", "band"), None)
    return jax.shard_map(local, mesh=mesh, in_specs=in_specs, out_specs=out_specs, check_vma=False)
```

```python
import functools

import jax
import jax.numpy as jnp
from jax import lax
from jax.experimental import pallas as pl
from jax.experimental.pallas import tpu as pltpu
from jax.sharding import PartitionSpec as P

LAGS = 256
NFFT = 2048
K0 = 64
OFFSET = 5
STEP = 8
GROUPS = (("down", 1), ("up", 1), ("up", 1), ("down", 1), ("up", 1), ("up", 1), ("down", 1), ("up", 1))
WHITEN = (2, 3, 3)
PLAN = (
    ("send", 0),
    ("send", 1),
    ("third", 1),
    ("send", 2),
    ("third", 2),
    ("send", 3),
    ("send", 4),
    ("third", 4),
    ("join", (0, 1), "t", "s"),
    ("send", 5, "v0"),
    ("third", 5, "v0"),
    ("join", (2, 4), "v0", "g3"),
    ("send", 7, "p0"),
    ("third", 7, "p0"),
    ("send", 6, "g5"),
    ("join", (5, 7), "v1", "p0"),
    ("join", (3, 6), "v2", "p1"),
)


def row_sums(x):
    ones = jnp.ones((x.shape[1], 128), jnp.bfloat16)
    high = x.astype(jnp.bfloat16)
    low = (x - high.astype(jnp.float32)).astype(jnp.bfloat16)
    return jnp.dot(high, ones, preferred_element_type=jnp.float32) + jnp.dot(
        low, ones, preferred_element_type=jnp.float32
    )


def whiten_kernel(starts, x_ref, live_ref, *o_refs):
    channels, windows = x_ref.shape[2:]
    step = pl.program_id(0)
    rows = lax.broadcasted_iota(jnp.int32, (channels, channels), 0)
    columns = lax.broadcasted_iota(jnp.int32, (channels, channels), 1)
    live = row_sums(jnp.where(rows == columns, live_ref[...].astype(jnp.float32), 0.0))

    def write(o_ref):
        for f in range(STEP):
            real = x_ref[0, f].astype(jnp.float32)
            imag = x_ref[1, f].astype(jnp.float32)
            power = row_sums(real * real + imag * imag) * (1.0 / windows)
            scale = live * lax.rsqrt(live * live * power + 1e-06)
            for lane in range(0, windows, 128):
                part = slice(lane, lane + 128)
                o_ref[f, 0, :, part] = (real[:, part] * scale).astype(jnp.bfloat16)
                o_ref[f, 1, :, part] = (imag[:, part] * scale).astype(jnp.bfloat16)

    for k, o_ref in enumerate(o_refs):
        pl.when((step >= starts[k]) & (step < starts[k + 1]))(functools.partial(write, o_ref))


def whiten(spectra, live, first, counts):
    _, _, channels, windows = spectra.shape
    steps = [count // STEP for count in counts]
    starts = [sum(steps[:k]) for k in range(len(steps) + 1)]

    def out_block(k):
        return lambda i: (jnp.clip(i - starts[k], 0, steps[k] - 1), 0, 0, 0)

    return pl.pallas_call(
        functools.partial(whiten_kernel, starts),
        grid=(starts[-1],),
        in_specs=[
            pl.BlockSpec((2, STEP, channels, windows), lambda i: (0, first // STEP + i, 0, 0)),
            pl.BlockSpec((1, channels), lambda i: (0, 0)),
        ],
        out_specs=[
            pl.BlockSpec((STEP, 2, channels, windows), out_block(k)) for k in range(len(counts))
        ],
        out_shape=[
            jax.ShapeDtypeStruct((count, 2, channels, windows), jnp.bfloat16) for count in counts
        ],
        cost_estimate=pl.CostEstimate(
            flops=16 * sum(counts) * channels * windows,
            bytes_accessed=8 * sum(counts) * channels * windows,
            transcendentals=0,
        ),
        name="whiten",
    )(spectra, live)


def cross_kernel(shapes, pick_ref, *refs):
    *refs, o_ref, acc = refs
    bands = o_ref.shape[0]
    place = 0
    for sources in shapes:
        x_ref, y_refs, refs = refs[0], refs[1 : 1 + sources], refs[1 + sources :]
        count, _, channels, windows = x_ref.shape
        depth = 2 * count
        for f in range(count):
            x = x_ref[f].reshape(2 * channels, windows)
            y = y_refs[0][f]
            if sources > 1:
                y = jnp.where(pick_ref[0] > 0, y_refs[1][f], y)
            y = y.reshape(2 * channels, windows)
            product = lax.dot_general(
                x, y, (((1,), (1,)), ((), ())), preferred_element_type=jnp.float32
            )
            low, high = product[:channels], product[channels:]
            real = low[:, :channels] + high[:, channels:]
            imag = high[:, :channels] - low[:, channels:]
            acc[pl.ds(f, channels, stride=depth), :] = real
            acc[pl.ds(count + f, channels, stride=depth), :] = imag
        rows = channels * depth // bands
        for band in range(bands):
            part = acc[band * rows : (band + 1) * rows, :]
            o_ref[band, place : place + rows, :] = part.astype(jnp.bfloat16)
        place += rows


def cross(groups, pick, bands):
    channels = groups[0][0].shape[2]
    rows = [channels * 2 * x.shape[0] for x, _ in groups]
    work = sum(x.size for x, _ in groups)
    return pl.pallas_call(
        functools.partial(cross_kernel, [len(ys) for _, ys in groups]),
        in_specs=[pl.BlockSpec(memory_space=pltpu.SMEM)]
        + [pl.BlockSpec(memory_space=pltpu.VMEM)] * sum(1 + len(ys) for _, ys in groups),
        out_shape=jax.ShapeDtypeStruct((bands, sum(rows) // bands, channels), jnp.bfloat16),
        scratch_shapes=[pltpu.VMEM((max(rows) + max(rows) // channels, channels), jnp.float32)],
        compiler_params=pltpu.CompilerParams(vmem_limit_bytes=40 * 1024 * 1024),
        cost_estimate=pl.CostEstimate(
            flops=4 * work * channels, bytes_accessed=5 * work, transcendentals=0
        ),
        name="cross",
    )(pick, *[ref for x, ys in groups for ref in (x, *ys)])


def lags_kernel(norm, places, *refs):
    *piece_refs, table_ref, o_ref = refs
    rows, channels = o_ref.shape[0], piece_refs[0].shape[2]
    for a in range(rows // channels):
        columns = []
        for ref, (place, depth) in zip(piece_refs, places):
            start = place + a * depth
            columns += [ref[band, start : start + depth, :] for band in range(ref.shape[0])]
        total = lax.dot_general(
            jnp.concatenate(columns, axis=0),
            table_ref[...],
            (((0,), (0,)), ((), ())),
            preferred_element_type=jnp.float32,
        )
        o_ref[a * channels : (a + 1) * channels, :] = (total * norm).astype(o_ref.dtype)


def to_lags(pieces, table, norm, dtype):
    bands, _, channels = pieces[0][0].shape
    pairs = channels * channels // bands
    lags = table.shape[1]
    return pl.pallas_call(
        functools.partial(lags_kernel, norm, [(place, depth) for _, place, depth in pieces]),
        out_shape=jax.ShapeDtypeStruct((pairs, lags), dtype),
        compiler_params=pltpu.CompilerParams(vmem_limit_bytes=32 * 1024 * 1024),
        cost_estimate=pl.CostEstimate(
            flops=2 * pairs * table.size,
            bytes_accessed=2 * pairs * table.shape[0] + 4 * pairs * lags,
            transcendentals=0,
        ),
        name="to_lags",
    )(*[piece for piece, _, _ in pieces], table)


def lag_table(first, count, bands, freq_local):
    band = jnp.arange(bands, dtype=jnp.int32)[:, None]
    freq = K0 + band * freq_local + first + jnp.arange(count, dtype=jnp.int32)
    lag_index = jnp.arange(LAGS, dtype=jnp.int32) - LAGS // 2
    phase = freq[..., None] * lag_index % NFFT
    angle = phase.astype(jnp.float32) * (2.0 * jnp.pi / NFFT)
    table = jnp.stack([jnp.cos(angle), -jnp.sin(angle)], axis=1)
    return table.reshape(-1, LAGS).astype(jnp.bfloat16)


def routes(blocks):
    behind, ahead, third, back = [], [], [], []
    for i in range(blocks):
        partner = (i + OFFSET) % blocks
        place = (partner, partner - 2, i + 1, partner + 2)[i % 4] % blocks
        behind.append((partner, i))
        ahead.append((i, place))
        back.append((place, i))
        if place != partner:
            third.append((partner, place))
    return behind, ahead, third, back


def local(spectra, live):
    _, freq_local, channels, windows = spectra.shape
    bands = lax.axis_size("band")
    behind, ahead, third, back = routes(lax.axis_size("pair"))
    norm = 1.0 / (float(freq_local * bands) ** 0.5 * float(windows) ** 0.5)
    mask = live[None, :]
    pick = (lax.axis_index("pair") % 4 != 1).astype(jnp.int32)[None]
    counts = [eighths * freq_local // 8 for _, eighths in GROUPS]
    firsts = [sum(counts[:k]) for k in range(len(counts))]

    def after(own, earlier):
        return lax.optimization_barrier((own, earlier))[0]

    white = []
    for members in WHITEN:
        source = after(spectra, white[-1]) if white else spectra
        white += whiten(source, mask, firsts[len(white)], counts[len(white) : len(white) + members])

    table = {
        way: jnp.concatenate(
            [
                lag_table(firsts[k], counts[k], bands, freq_local)
                for kind, what, *_ in PLAN
                if kind == "join"
                for k in what
                if GROUPS[k][0] == way
            ]
        )
        for way in ("up", "down")
    }
    there = {"t": table["up"], "s": table["down"]}
    arrived = {}
    pieces = {"up": [], "down": []}
    for kind, what, *needs in PLAN:
        if kind != "join":
            way, own = GROUPS[what][0], white[what]
            sent = own
            for need in needs:
                sent = after(sent, there[need])
            if kind == "third":
                moved = there[f"y{what}"] = lax.ppermute(sent, "pair", third)
                arrived.setdefault(what, [own, [own]])[1].append(moved)
            elif way == "up":
                moved = there[f"g{what}"] = lax.ppermute(sent, "pair", ahead)
                arrived.setdefault(what, [own, [own]])[0] = moved
            else:
                moved = there[f"g{what}"] = lax.ppermute(sent, "pair", behind)
                arrived[what] = [own, [moved]]
            continue
        factors = [arrived[k] for k in what]
        for need in needs:
            factors[0] = [after(factors[0][0], there[need]), factors[0][1]]
        value = cross(factors, pick, bands)
        piece = lax.all_to_all(value, "band", 0, 0)
        number = sum(name[0] == "v" for name in there)
        there[f"v{number}"], there[f"p{number}"] = value, piece
        place = 0
        for k in what:
            way = GROUPS[k][0]
            pieces[way].append((piece, place, 2 * counts[k]))
            place += channels // bands * 2 * counts[k]
    far = to_lags(pieces["up"], table["up"], norm, jnp.bfloat16)
    far = lax.ppermute(far, "pair", back)
    near = to_lags(pieces["down"], table["down"], norm, jnp.float32)
    return near + far.astype(jnp.float32)


def solution(mesh):
    in_specs = (P(None, "band", "pair", None), P("pair"))
    out_specs = P(("pair", "band"), None)
    return jax.shard_map(local, mesh=mesh, in_specs=in_specs, out_specs=out_specs, check_vma=False)
```
